32 devices in a mesh: tm: 8 (over z, y), space: 4 (over x, core).
Axes of the slice: x: 2, y: 2, z: 4, core: 2. Of those that a mesh axis runs over, the one named last changes fastest.
Arguments:
- snapshots: bfloat16 [4096, 3, 4096], P('tm', None, 'space'), may hold values from -6 to 6
- cell_weights: float32 [4096], P('space'), may hold values from 0.25 to 4
- triads: int32 [64, 3], replicated, may hold values from 0 to 127, as said below
- owner_slots: int32 [8, 16], replicated, may hold values from -1 to 63, as said below
Outputs:
- bispectra: float32 [128, 512], P(('tm', 'space'))
The draws below stay inside these ranges and needn't reach their ends.
Inputs may be any that keep to these rules, and one draw needn't show every extreme that they name: `triads`: every row is (k, l, k + l); all three entries are below 128. `owner_slots`: every triad index stands in exactly one slot of the table; in each row the used slots come first and the others hold -1; some owner fills all 16 slots.
All inputs are finite; a program needn't handle non-finite values.
Results may differ from the reference program's by a relative error of at most 0.0076.
Values may be sent and summed in bfloat16 or wider, within the bound.
A program may use at most 64 MiB of HBM per device.

```python
import math
import jax
import jax.numpy as jnp
from jax import lax

NB = 16
NT = 256
K = 128
NSNAP = 4096
CPD = 128
NCELLS = 4096
TRI_OWN = 8
OWNERS = 8
NTRI = 64
SLOTS = 16


def draw_triads(key, part):
    draw_one = jax.random.randint(jax.random.fold_in(key, 21), (NTRI,), 0, K)
    draw_two = jax.random.randint(jax.random.fold_in(key, 22), (NTRI,), 0, K)
    folded = draw_one + draw_two >= K
    freq_one = jnp.where(folded, K - 1 - draw_one, draw_one)
    freq_two = jnp.where(folded, K - 1 - draw_two, draw_two)
    return jnp.stack([freq_one, freq_two, freq_one + freq_two], axis=1).astype(jnp.int32)


def draw_owner_slots(key, part):
    group_total = OWNERS // 4
    owner_order = jax.random.permutation(jax.random.fold_in(key, 31), OWNERS)
    shifts = jax.random.randint(jax.random.fold_in(key, 32), (group_total,), 0, TRI_OWN // 2 + 1)
    shifts = shifts.at[0].set(TRI_OWN // 2)
    pattern = jnp.array([2, 2, -2, -2], jnp.int32)
    placed = (TRI_OWN + shifts[:, None] * pattern[None, :]).reshape(OWNERS)
    owner_loads = jnp.zeros((OWNERS,), jnp.int32).at[owner_order].set(placed)
    starts = jnp.cumsum(owner_loads) - owner_loads
    triad_order = jax.random.permutation(jax.random.fold_in(key, 33), NTRI).astype(jnp.int32)
    slot_ids = jnp.arange(SLOTS, dtype=jnp.int32)
    position = jnp.clip(starts[:, None] + slot_ids[None, :], 0, NTRI - 1)
    used = slot_ids[None, :] < owner_loads[:, None]
    return jnp.where(used, triad_order[position], -1).astype(jnp.int32)


def block_levels(stream_key, shape, split, smallest, top_value):
    level = 1.0
    for dim, parts in split:
        steps = jax.random.uniform(jax.random.fold_in(jax.random.fold_in(stream_key, 6), dim), (parts,), jnp.float32, smallest / len(split), top_value / len(split))
        level = level * jnp.repeat(jnp.exp(steps), shape[dim] // parts).reshape((-1,) + (1,) * (len(shape) - 1 - dim))
    return level


def scatter_about(stream_key, extent, deviation, bound, cuts=(), kind=jnp.bfloat16):
    values = jax.random.normal(stream_key, extent, jnp.float32) * deviation
    if len(cuts) > 0:
        values = block_levels(stream_key, extent, cuts, -0.22, 0.18) * values
    return jnp.clip(values, min=-bound, max=bound).astype(kind)


def setup_inputs(seed: int = 0) -> dict:
    streams_of = jax.random.split(jax.random.key(seed), 5)
    return {
        "snapshots": scatter_about(streams_of[0], (NSNAP, 3, NCELLS), 1.0, 6.0, ((0, 8), (2, 4))),
        "cell_weights": jnp.clip(jnp.exp(math.log(4.0) - 2.7725887 * jax.random.uniform(streams_of[1], (NCELLS,), jnp.float32) ** block_levels(streams_of[1], (NCELLS,), ((0, 4),), -0.2, 0.2)), 0.25, 4.0),
        "triads": draw_triads(jax.random.fold_in(streams_of[4], 71), 0),
        "owner_slots": draw_owner_slots(jax.random.fold_in(streams_of[4], 71), 0),
    }


def spectral_table():
    sample = jnp.arange(NT, dtype=jnp.int32)
    freq_bins = jnp.arange(K, dtype=jnp.int32)
    phase_idx = freq_bins[:, None] * sample[None, :] % NT
    angles = 2.0 * math.pi / NT * phase_idx.astype(jnp.float32)
    window = 0.5 - 0.5 * jnp.cos(2.0 * math.pi / NT * sample.astype(jnp.float32))
    norm_scale = math.sqrt(8.0 / (3.0 * NT))
    real_rows = norm_scale * window[None, :] * jnp.cos(angles)
    imag_rows = -norm_scale * window[None, :] * jnp.sin(angles)
    return jnp.stack([real_rows, imag_rows]).astype(jnp.bfloat16)

def triad_terms(spectra, weight_rows, triads, triad_index):
    triad_freqs = jnp.take(triads, triad_index, axis=0)
    first_spec = jnp.take(spectra, triad_freqs[:, 0], axis=1).astype(jnp.float32)
    second_spec = jnp.take(spectra, triad_freqs[:, 1], axis=1).astype(jnp.float32)
    third_spec = jnp.take(spectra, triad_freqs[:, 2], axis=1).astype(jnp.float32)
    prod_real = (first_spec[0] * second_spec[0] - first_spec[1] * second_spec[1]) * weight_rows
    prod_imag = (first_spec[0] * second_spec[1] + first_spec[1] * second_spec[0]) * weight_rows
    product = jnp.stack([prod_real, prod_imag]).astype(jnp.bfloat16).astype(jnp.float32)
    gram = jnp.einsum('rtbc,stdc->trbsd', product, third_spec)
    bis_real = gram[:, 0, :, 0, :] + gram[:, 1, :, 1, :]
    bis_imag = gram[:, 0, :, 1, :] - gram[:, 1, :, 0, :]
    return jnp.stack([bis_real, bis_imag], axis=1).reshape(triad_index.shape[0], 2 * NB * NB)

def reference(snapshots, cell_weights, triads, owner_slots):
    dft_table = spectral_table().astype(jnp.float32)
    weight_scale = 1.0 / math.sqrt(3.0 * NCELLS)
    all_triads = jnp.arange(NTRI, dtype=jnp.int32)

    def accumulate(carry, group_index):
        first_cell = (group_index * CPD).astype(jnp.int32)
        local_snap = lax.dynamic_slice_in_dim(snapshots, first_cell, CPD, 2)
        local_w = lax.dynamic_slice_in_dim(cell_weights, first_cell, CPD, 0) * weight_scale
        blocks = local_snap.reshape(NB, NT, 3 * CPD).astype(jnp.float32)
        spectra = jnp.einsum('rkn,bnc->rkbc', dft_table, blocks).astype(jnp.bfloat16)
        weight_rows = jnp.tile(local_w, 3)
        return (carry + triad_terms(spectra, weight_rows, triads, all_triads), None)
    start_sums = jnp.zeros((NTRI, 2 * NB * NB), jnp.float32)
    triad_sums, unused_out = lax.scan(accumulate, start_sums, jnp.arange(NCELLS // CPD, dtype=jnp.int32))
    flat_slots = owner_slots.reshape(-1)
    filled = (flat_slots >= 0).astype(jnp.float32)
    chosen = jnp.take(triad_sums, jnp.maximum(flat_slots, 0).astype(jnp.int32), axis=0)
    return chosen * filled[:, None]
```

```python
import functools
import math

import jax
import jax.numpy as jnp
import ml_dtypes
import numpy as np
from jax import lax
from jax.experimental import pallas as pl
from jax.experimental.pallas import tpu as pltpu
from jax.sharding import PartitionSpec as P

NB = 16
NT = 256
K = 128
GROUP = 8
LANES = 128
MESH = pl.DeviceIdType.MESH


def spectral_table():
    sample = np.arange(NT)
    freq_bins = np.arange(K)
    angles = 2.0 * math.pi / NT * (freq_bins[:, None] * sample[None, :] % NT)
    window = 0.5 - 0.5 * np.cos(2.0 * math.pi / NT * sample)
    scale = math.sqrt(8.0 / (3.0 * NT))
    rows = np.stack(
        [scale * window * np.cos(angles), -scale * window * np.sin(angles)], axis=1
    )
    return rows.reshape(2 * K, NT).astype(np.float32).astype(ml_dtypes.bfloat16)


def kernel(
    n,
    ns,
    weight_scale,
    snap,
    table,
    weights,
    freqs,
    out,
    recv,
    rows,
    spec,
    narrow,
    acc,
    part,
    summed,
    last,
    send_sem,
    recv_sem,
    own_sem,
    send1,
    recv1,
    send2,
    recv2,
):
    comps, times = snap.shape[0], snap.shape[1]
    me = lax.axis_index("tm")
    col = lax.axis_index("space")

    barrier = pltpu.get_barrier_semaphore()

    def greet_tm(off, carry):
        pl.semaphore_signal(
            barrier, inc=1, device_id=(lax.rem(me + off, n), col), device_id_type=MESH
        )
        return carry

    lax.fori_loop(1, n, greet_tm, 0)
    for off in range(1, ns):
        pl.semaphore_signal(
            barrier, inc=1, device_id=(me, lax.rem(col + off, ns)), device_id_type=MESH
        )
    pl.semaphore_wait(barrier, n - 1 + ns - 1)

    def exchange(c, off):
        peer = lax.rem(me + off, n)
        return pltpu.make_async_remote_copy(
            src_ref=snap.at[c, :, pl.ds(pl.multiple_of(peer * LANES, LANES), LANES)],
            dst_ref=recv.at[c, pl.ds(pl.multiple_of(me * times, 16), times), :],
            send_sem=send_sem.at[c, off],
            recv_sem=recv_sem.at[c, off],
            device_id=(peer, col),
            device_id_type=MESH,
        )

    def own(c):
        return pltpu.make_async_copy(
            snap.at[c, :, pl.ds(pl.multiple_of(me * LANES, LANES), LANES)],
            recv.at[c, pl.ds(pl.multiple_of(me * times, 16), times), :],
            own_sem.at[c],
        )

    for c in range(comps):

        def begin(off, carry, c=c):
            exchange(c, off).start()
            return carry

        lax.fori_loop(1, n, begin, 0)
        own(c).start()

    w_row = weights[pl.ds(me, 1), :] * weight_scale
    lane = lax.broadcasted_iota(jnp.int32, (2 * NB, 2 * LANES), 1)
    lane_group = lax.rem(lane, LANES) // NB
    low = lax.broadcasted_iota(jnp.int32, (NB, LANES), 1) < LANES // 2
    groups = freqs.shape[1] // GROUP
    per_owner = groups // n

    def dft(c, b):
        x = recv[c, pl.ds(pl.multiple_of(b * NT, NT), NT), :]
        y = jnp.dot(table[...], x, preferred_element_type=jnp.float32)
        rows[pl.ds(b, 2 * K, stride=NB), :] = y

    def regroup(k, carry):
        both = rows[pl.ds(pl.multiple_of(k * 2 * NB, 2 * NB), 2 * NB), :].astype(jnp.bfloat16)
        narrow[k] = both
        spec[k] = both.astype(jnp.float32)
        return carry

    def gram_group(c, g):
        owner = g // per_owner
        half = lax.rem(g, per_owner)
        prods, c_re, c_im = [], [], []
        for s in range(GROUP):
            place = g * GROUP + s
            a = spec[freqs[0, place]]
            b2 = spec[freqs[1, place]]
            c2 = narrow[freqs[2, place]]
            re = (a[:NB] * b2[:NB] - a[NB:] * b2[NB:]) * w_row
            im = (a[:NB] * b2[NB:] + a[NB:] * b2[:NB]) * w_row
            prods += [re.astype(jnp.bfloat16), im.astype(jnp.bfloat16)]
            c_re.append(c2[:NB])
            c_im.append(c2[NB:])
        left = jnp.concatenate(prods, axis=0)
        right = jnp.concatenate(c_re + c_im, axis=0)
        gram = lax.dot_general(
            left, right, (((1,), (1,)), ((), ())), preferred_element_type=jnp.float32
        )
        diag = gram[: 2 * NB]
        for s in range(1, GROUP):
            diag = jnp.where(lane_group == s, gram[2 * NB * s : 2 * NB * (s + 1)], diag)
        real = diag[:NB, :LANES] + diag[NB:, LANES:]
        imag = diag[:NB, LANES:] - diag[NB:, :LANES]
        half_turn = LANES // 2
        first = jnp.where(low, real, pltpu.roll(imag, half_turn, 1))
        second = jnp.where(low, pltpu.roll(real, half_turn, 1), imag)
        if c == 0:
            acc[2 * half, owner] = first
            acc[2 * half + 1, owner] = second
        else:
            acc[2 * half, owner] += first
            acc[2 * half + 1, owner] += second

    for c in range(comps):
        own(c).wait()
        if times % NT == 0:

            def transform(i, carry, c=c):
                dft(c, me * (times // NT) + i)
                return carry

            lax.fori_loop(0, times // NT, transform, 0)

            def arrive(off, carry, c=c):
                exchange(c, off).wait_recv()
                src = lax.rem(me - off + n, n)
                for i in range(times // NT):
                    dft(c, src * (times // NT) + i)
                return carry

            lax.fori_loop(1, n, arrive, 0)
        else:

            def arrive(off, carry, c=c):
                exchange(c, off).wait_recv()
                return carry

            lax.fori_loop(1, n, arrive, 0)

            def transform(b, carry, c=c):
                dft(c, b)
                return carry

            lax.fori_loop(0, NB, transform, 0)

        lax.fori_loop(0, K, regroup, 0, unroll=4)

        def grams(g, carry, c=c):
            gram_group(c, g)
            return carry

        lax.fori_loop(0, groups, grams, 0)

    def across(off):
        peer = lax.rem(col + off, ns)
        return pltpu.make_async_remote_copy(
            src_ref=acc.at[peer],
            dst_ref=part.at[off - 1],
            send_sem=send1.at[off - 1],
            recv_sem=recv1.at[off - 1],
            device_id=(me, peer),
            device_id_type=MESH,
        )

    for off in range(1, ns):
        across(off).start()
    for off in range(1, ns):
        across(off).wait_recv()
    total = acc[col]
    for off in range(1, ns):
        total = total + part[off - 1]
    summed[...] = total

    def along(off):
        peer = lax.rem(me + off, n)
        return pltpu.make_async_remote_copy(
            src_ref=summed.at[peer],
            dst_ref=last.at[off],
            send_sem=send2.at[off],
            recv_sem=recv2.at[off],
            device_id=(peer, col),
            device_id_type=MESH,
        )

    def begin2(off, carry):
        along(off).start()
        return carry

    lax.fori_loop(1, n, begin2, 0)

    def add2(off, total):
        along(off).wait_recv()
        return total + last[off]

    out[...] = lax.fori_loop(1, n, add2, summed[me])

    for off in range(1, ns):
        across(off).wait_send()

    def drain(off, carry):
        for c in range(comps):
            exchange(c, off).wait_send()
        along(off).wait_send()
        return carry

    lax.fori_loop(1, n, drain, 0)


def shards(n, ns, snapshots, cell_weights, triads, owner_slots):
    times, comps, cells = snapshots.shape
    owners, slot_count = owner_slots.shape
    weight_scale = 1.0 / math.sqrt(comps * cells * ns)
    vmem = pl.BlockSpec(memory_space=pltpu.VMEM)
    smem = pl.BlockSpec(memory_space=pltpu.SMEM)
    anywhere = pl.BlockSpec(memory_space=pl.ANY)
    sem = pltpu.SemaphoreType.DMA
    tile = pl.pallas_call(
        functools.partial(kernel, n, ns, weight_scale),
        out_shape=jax.ShapeDtypeStruct((NB, LANES), jnp.float32),
        in_specs=[anywhere, vmem, vmem, smem],
        out_specs=vmem,
        scratch_shapes=[
            pltpu.VMEM((comps, NB * NT, LANES), jnp.bfloat16),
            pltpu.VMEM((2 * K * NB, LANES), jnp.float32),
            pltpu.VMEM((K, 2 * NB, LANES), jnp.float32),
            pltpu.VMEM((K, 2 * NB, LANES), jnp.bfloat16),
            pltpu.VMEM((ns, n, NB, LANES), jnp.float32),
            pltpu.VMEM((ns - 1, n, NB, LANES), jnp.float32),
            pltpu.VMEM((n, NB, LANES), jnp.float32),
            pltpu.VMEM((n, NB, LANES), jnp.float32),
            sem((comps, n)),
            sem((comps, n)),
            sem((comps,)),
            sem((ns - 1,)),
            sem((ns - 1,)),
            sem((n,)),
            sem((n,)),
        ],
        compiler_params=pltpu.CompilerParams(
            collective_id=0, has_side_effects=True, vmem_limit_bytes=40 * 1024 * 1024
        ),
    )(
        snapshots.transpose(1, 0, 2),
        jnp.asarray(spectral_table()),
        cell_weights.reshape(n, LANES),
        jnp.take(triads.T, jnp.maximum(owner_slots, 0).reshape(-1), axis=1, mode="clip"),
    )
    mine = slot_count // ns
    flat = tile.reshape(NB, 2, mine, NB).transpose(2, 1, 0, 3).reshape(mine, 2 * NB * NB)
    my_slots = lax.dynamic_slice(
        owner_slots, (lax.axis_index("tm"), lax.axis_index("space") * mine), (1, mine)
    ).reshape(mine, 1)
    return jnp.where(my_slots >= 0, flat, 0.0)


def solution(mesh):
    placed = (P("tm", None, "space"), P("space"), P(), P())
    n, ns = mesh.shape["tm"], mesh.shape["space"]
    return jax.shard_map(
        functools.partial(shards, n, ns),
        mesh=mesh,
        in_specs=placed,
        out_specs=P(("tm", "space"), None),
        check_vma=False,
    )
```

```python
import functools
import math

import jax
import jax.numpy as jnp
import ml_dtypes
import numpy as np
from jax import lax
from jax.experimental import pallas as pl
from jax.experimental.pallas import tpu as pltpu
from jax.sharding import PartitionSpec as P

NB = 16
NT = 256
K = 128
GROUP = 8
LANES = 128
MESH = pl.DeviceIdType.MESH


def spectral_table():
    sample = np.arange(NT)
    freq_bins = np.arange(K)
    angles = 2.0 * math.pi / NT * (freq_bins[:, None] * sample[None, :] % NT)
    window = 0.5 - 0.5 * np.cos(2.0 * math.pi / NT * sample)
    scale = math.sqrt(8.0 / (3.0 * NT))
    rows = np.stack(
        [scale * window * np.cos(angles), -scale * window * np.sin(angles)], axis=1
    )
    return rows.reshape(2 * K, NT).astype(np.float32).astype(ml_dtypes.bfloat16)


def choose(table, triads, slot_row, chosen, freqs, count):
    wide = 2 * K
    ntri = triads.shape[1]
    nslot = slot_row.shape[1]
    bin_of = lax.broadcasted_iota(jnp.int32, (wide, ntri), 0) // 2
    hit = (triads[0:1] == bin_of) | (triads[1:2] == bin_of) | (triads[2:3] == bin_of)
    hit = jnp.where(hit, 1.0, 0.0).astype(jnp.bfloat16)
    ones = jnp.ones((16, ntri), jnp.bfloat16)
    hits = lax.dot_general(
        ones, hit, (((1,), (1,)), ((), ())), preferred_element_type=jnp.float32
    )
    used = jnp.where(hits > 0.5, 1.0, 0.0)
    row = lax.broadcasted_iota(jnp.int32, (wide, wide), 0)
    column = lax.broadcasted_iota(jnp.int32, (wide, wide), 1)
    before = jnp.where(row < column, 1.0, 0.0).astype(jnp.bfloat16)
    rank = jnp.dot(used.astype(jnp.bfloat16), before, preferred_element_type=jnp.float32)
    place = jnp.where(used > 0.5, rank, -1.0)[0:1].astype(jnp.int32)
    pick = jnp.where(row == place, 1.0, 0.0).astype(jnp.bfloat16)
    chosen[...] = jnp.dot(
        pick, table[...], preferred_element_type=jnp.float32
    ).astype(jnp.bfloat16)
    triad_row = lax.broadcasted_iota(jnp.int32, (ntri, nslot), 0)
    of_slot = jnp.where(triad_row == slot_row[...], 1.0, 0.0).astype(jnp.bfloat16)
    bin_row = lax.broadcasted_iota(jnp.int32, (wide, nslot), 0)
    rank = rank.astype(jnp.bfloat16)
    for i in range(3):
        tri = jnp.broadcast_to(triads[i : i + 1].astype(jnp.float32), (16, ntri))
        freq = jnp.dot(
            tri.astype(jnp.bfloat16), of_slot, preferred_element_type=jnp.float32
        )
        same = bin_row == 2 * freq[0:1].astype(jnp.int32)
        same = jnp.where(same, 1.0, 0.0).astype(jnp.bfloat16)
        twice = jnp.dot(rank, same, preferred_element_type=jnp.float32)
        freqs[i : i + 1, :] = (twice[0:1] * 0.5).astype(jnp.int32)
    count[0, 0] = (jnp.sum(used[0:1]) * 0.5).astype(jnp.int32)


def kernel(
    n,
    ns,
    weight_scale,
    bins,
    snap,
    table,
    weights,
    freqs,
    out,
    local,
    stage,
    recv,
    rows,
    spec,
    narrow,
    acc,
    part,
    summed,
    last,
    send_sem,
    recv_sem,
    own_sem,
    send1,
    recv1,
    send2,
    recv2,
):
    comps, times = snap.shape[0], snap.shape[1]
    me = lax.axis_index("tm")
    col = lax.axis_index("space")
    first = times % NT == 0
    blocks = times // NT

    def load(c):
        return pltpu.make_async_copy(snap.at[c], local.at[c], own_sem.at[c])

    if first:
        for c in range(comps):
            load(c).start()

    barrier = pltpu.get_barrier_semaphore()

    def greet_tm(off, carry):
        pl.semaphore_signal(
            barrier, inc=1, device_id=(lax.rem(me + off, n), col), device_id_type=MESH
        )
        return carry

    lax.fori_loop(1, n, greet_tm, 0)
    for off in range(1, ns):
        pl.semaphore_signal(
            barrier, inc=1, device_id=(me, lax.rem(col + off, ns)), device_id_type=MESH
        )
    pl.semaphore_wait(barrier, n - 1 + ns - 1)

    def exchange(c, off):
        peer = lax.rem(me + off, n)
        if first:
            return pltpu.make_async_remote_copy(
                src_ref=stage.at[c, off],
                dst_ref=recv.at[c, off],
                send_sem=send_sem.at[c, off],
                recv_sem=recv_sem.at[c, off],
                device_id=(peer, col),
                device_id_type=MESH,
            )
        return pltpu.make_async_remote_copy(
            src_ref=snap.at[c, :, pl.ds(pl.multiple_of(peer * LANES, LANES), LANES)],
            dst_ref=recv.at[c, pl.ds(pl.multiple_of(me * times, 16), times), :],
            send_sem=send_sem.at[c, off],
            recv_sem=recv_sem.at[c, off],
            device_id=(peer, col),
            device_id_type=MESH,
        )

    def own(c):
        return pltpu.make_async_copy(
            snap.at[c, :, pl.ds(pl.multiple_of(me * LANES, LANES), LANES)],
            recv.at[c, pl.ds(pl.multiple_of(me * times, 16), times), :],
            own_sem.at[c],
        )

    def spectra(c, off):
        peer = lax.rem(me + off, n)
        for i in range(blocks):
            x = local[
                c, i * NT : (i + 1) * NT, pl.ds(pl.multiple_of(peer * LANES, LANES), LANES)
            ]
            y = jnp.dot(table[: 2 * bins], x, preferred_element_type=jnp.float32)
            stage[c, off, i] = y.astype(jnp.bfloat16)

    for c in range(comps):
        if first:
            load(c).wait()

        def begin(off, carry, c=c):
            if first:
                spectra(c, off)
            exchange(c, off).start()
            return carry

        lax.fori_loop(1, n, begin, 0)
        if not first:
            own(c).start()

    w_row = weights[pl.ds(me, 1), :] * weight_scale
    lane = lax.broadcasted_iota(jnp.int32, (2 * NB, 2 * LANES), 1)
    lane_group = lax.rem(lane, LANES) // NB
    low = lax.broadcasted_iota(jnp.int32, (NB, LANES), 1) < LANES // 2
    groups = freqs.shape[1] // GROUP
    per_owner = groups // n

    def dft(c, b):
        x = recv[c, pl.ds(pl.multiple_of(b * NT, NT), NT), :]
        y = jnp.dot(table[...], x, preferred_element_type=jnp.float32)
        rows[pl.ds(b, 2 * K, stride=NB), :] = y

    def regroup(k, carry):
        both = rows[pl.ds(pl.multiple_of(k * 2 * NB, 2 * NB), 2 * NB), :].astype(jnp.bfloat16)
        narrow[k] = both
        spec[k] = both.astype(jnp.float32)
        return carry

    def spread(c, off, source):
        src = lax.rem(me - off + n, n)
        for i in range(blocks):
            rows[pl.ds(src * blocks + i, 2 * bins, stride=NB), :] = source[c, off, i].astype(
                jnp.float32
            )

    def gram_group(c, g):
        owner = g // per_owner
        half = lax.rem(g, per_owner)
        prods, c_re, c_im = [], [], []
        for s in range(GROUP):
            place = g * GROUP + s
            a = spec[freqs[0, place]]
            b2 = spec[freqs[1, place]]
            c2 = narrow[freqs[2, place]]
            re = (a[:NB] * b2[:NB] - a[NB:] * b2[NB:]) * w_row
            im = (a[:NB] * b2[NB:] + a[NB:] * b2[:NB]) * w_row
            prods += [re.astype(jnp.bfloat16), im.astype(jnp.bfloat16)]
            c_re.append(c2[:NB])
            c_im.append(c2[NB:])
        left = jnp.concatenate(prods, axis=0)
        right = jnp.concatenate(c_re + c_im, axis=0)
        gram = lax.dot_general(
            left, right, (((1,), (1,)), ((), ())), preferred_element_type=jnp.float32
        )
        diag = gram[: 2 * NB]
        for s in range(1, GROUP):
            diag = jnp.where(lane_group == s, gram[2 * NB * s : 2 * NB * (s + 1)], diag)
        real = diag[:NB, :LANES] + diag[NB:, LANES:]
        imag = diag[:NB, LANES:] - diag[NB:, :LANES]
        half_turn = LANES // 2
        even = jnp.where(low, real, pltpu.roll(imag, half_turn, 1))
        odd = jnp.where(low, pltpu.roll(real, half_turn, 1), imag)
        if c == 0:
            acc[2 * half, owner] = even
            acc[2 * half + 1, owner] = odd
        else:
            acc[2 * half, owner] += even
            acc[2 * half + 1, owner] += odd

    for c in range(comps):
        if first:
            spectra(c, 0)
            spread(c, 0, stage)

            def arrive(off, carry, c=c):
                exchange(c, off).wait_recv()
                spread(c, off, recv)
                return carry

            lax.fori_loop(1, n, arrive, 0)
        else:
            own(c).wait()

            def arrive(off, carry, c=c):
                exchange(c, off).wait_recv()
                return carry

            lax.fori_loop(1, n, arrive, 0)

            def transform(b, carry, c=c):
                dft(c, b)
                return carry

            lax.fori_loop(0, NB, transform, 0)

        lax.fori_loop(0, bins, regroup, 0, unroll=4)

        def grams(g, carry, c=c):
            gram_group(c, g)
            return carry

        lax.fori_loop(0, groups, grams, 0)

    def across(off):
        peer = lax.rem(col + off, ns)
        return pltpu.make_async_remote_copy(
            src_ref=acc.at[peer],
            dst_ref=part.at[off - 1],
            send_sem=send1.at[off - 1],
            recv_sem=recv1.at[off - 1],
            device_id=(me, peer),
            device_id_type=MESH,
        )

    for off in range(1, ns):
        across(off).start()
    for off in range(1, ns):
        across(off).wait_recv()
    total = acc[col]
    for off in range(1, ns):
        total = total + part[off - 1]
    summed[...] = total

    def along(off):
        peer = lax.rem(me + off, n)
        return pltpu.make_async_remote_copy(
            src_ref=summed.at[peer],
            dst_ref=last.at[off],
            send_sem=send2.at[off],
            recv_sem=recv2.at[off],
            device_id=(peer, col),
            device_id_type=MESH,
        )

    def begin2(off, carry):
        along(off).start()
        return carry

    lax.fori_loop(1, n, begin2, 0)

    def add2(off, total):
        along(off).wait_recv()
        return total + last[off]

    out[...] = lax.fori_loop(1, n, add2, summed[me])

    for off in range(1, ns):
        across(off).wait_send()

    def drain(off, carry):
        for c in range(comps):
            exchange(c, off).wait_send()
        along(off).wait_send()
        return carry

    lax.fori_loop(1, n, drain, 0)


def shards(n, ns, snapshots, cell_weights, triads, owner_slots):
    times, comps, cells = snapshots.shape
    owners, slot_count = owner_slots.shape
    weight_scale = 1.0 / math.sqrt(comps * cells * ns)
    vmem = pl.BlockSpec(memory_space=pltpu.VMEM)
    smem = pl.BlockSpec(memory_space=pltpu.SMEM)
    anywhere = pl.BlockSpec(memory_space=pl.ANY)
    sem = pltpu.SemaphoreType.DMA
    first = times % NT == 0
    blocks = times // NT

    def call(which, bins, *operands):
        if first:
            local = pltpu.VMEM((comps, times, n * LANES), jnp.bfloat16)
            stage = pltpu.VMEM((comps, n, blocks, 2 * bins, LANES), jnp.bfloat16)
            recv = stage
        else:
            local = stage = pltpu.VMEM((16, LANES), jnp.bfloat16)
            recv = pltpu.VMEM((comps, NB * NT, LANES), jnp.bfloat16)
        return pl.pallas_call(
            functools.partial(kernel, n, ns, weight_scale, bins),
            out_shape=jax.ShapeDtypeStruct((NB, LANES), jnp.float32),
            in_specs=[anywhere, vmem, vmem, smem],
            out_specs=vmem,
            scratch_shapes=[
                local,
                stage,
                recv,
                pltpu.VMEM((2 * bins * NB, LANES), jnp.float32),
                pltpu.VMEM((bins, 2 * NB, LANES), jnp.float32),
                pltpu.VMEM((bins, 2 * NB, LANES), jnp.bfloat16),
                pltpu.VMEM((ns, n, NB, LANES), jnp.float32),
                pltpu.VMEM((ns - 1, n, NB, LANES), jnp.float32),
                pltpu.VMEM((n, NB, LANES), jnp.float32),
                pltpu.VMEM((n, NB, LANES), jnp.float32),
                sem((comps, n)),
                sem((comps, n)),
                sem((comps,)),
                sem((ns - 1,)),
                sem((ns - 1,)),
                sem((n,)),
                sem((n,)),
            ],
            compiler_params=pltpu.CompilerParams(
                collective_id=which,
                has_side_effects=True,
                vmem_limit_bytes=58 * 1024 * 1024,
            ),
        )(*operands)

    table = jnp.asarray(spectral_table())
    snap = snapshots.transpose(1, 0, 2)
    weights = cell_weights.reshape(n, LANES)
    flat_slots = owner_slots.reshape(1, -1)
    if first:
        sizes = (96, 104, K)
        chosen, freqs, count = pl.pallas_call(
            choose,
            out_shape=(
                jax.ShapeDtypeStruct((2 * K, NT), jnp.bfloat16),
                jax.ShapeDtypeStruct((3, flat_slots.shape[1]), jnp.int32),
                jax.ShapeDtypeStruct((1, 1), jnp.int32),
            ),
            in_specs=[vmem, vmem, vmem],
            out_specs=(vmem, vmem, smem),
        )(table, triads.T, flat_slots)
        need = count[0, 0]
        which = (need > sizes[0]).astype(jnp.int32) + (need > sizes[1]).astype(jnp.int32)
        tile = lax.switch(
            which,
            [functools.partial(call, i, bins) for i, bins in enumerate(sizes)],
            snap,
            chosen,
            weights,
            freqs,
        )
    else:
        freqs = jnp.take(triads.T, jnp.maximum(flat_slots[0], 0), axis=1, mode="clip")
        tile = call(0, K, snap, table, weights, freqs)
    mine = slot_count // ns
    flat = tile.reshape(NB, 2, mine, NB).transpose(2, 1, 0, 3).reshape(mine, 2 * NB * NB)
    my_slots = lax.dynamic_slice(
        owner_slots, (lax.axis_index("tm"), lax.axis_index("space") * mine), (1, mine)
    ).reshape(mine, 1)
    return jnp.where(my_slots >= 0, flat, 0.0)


def solution(mesh):
    placed = (P("tm", None, "space"), P("space"), P(), P())
    n, ns = mesh.shape["tm"], mesh.shape["space"]
    return jax.shard_map(
        functools.partial(shards, n, ns),
        mesh=mesh,
        in_specs=placed,
        out_specs=P(("tm", "space"), None),
        check_vma=False,
    )
```

```python
import functools
import math

import jax
import jax.numpy as jnp
import ml_dtypes
import numpy as np
from jax import lax
from jax.experimental import pallas as pl
from jax.experimental.pallas import tpu as pltpu
from jax.sharding import PartitionSpec as P

NB = 16
NT = 256
K = 128
GROUP = 8
LANES = 128
MESH = pl.DeviceIdType.MESH


def spectral_table():
    sample = np.arange(NT)
    freq_bins = np.arange(K)
    angles = 2.0 * math.pi / NT * (freq_bins[:, None] * sample[None, :] % NT)
    window = 0.5 - 0.5 * np.cos(2.0 * math.pi / NT * sample)
    scale = math.sqrt(8.0 / (3.0 * NT))
    rows = np.stack(
        [scale * window * np.cos(angles), -scale * window * np.sin(angles)], axis=1
    )
    return rows.reshape(2 * K, NT).astype(np.float32).astype(ml_dtypes.bfloat16)


def choose(ns, table, triads, slots, chosen, freqs, filled, count):
    wide = 2 * K
    ntri = triads.shape[1]
    owners, per = slots.shape
    nslot = owners * per
    mine = per // ns
    slot_of = lax.broadcasted_iota(jnp.int32, (per, nslot), 0)
    lane = lax.broadcasted_iota(jnp.int32, (per, nslot), 1)
    repeat = jnp.where(lane % per == slot_of, 1.0, 0.0).astype(jnp.bfloat16)
    held = slots[...].astype(jnp.float32)
    wide_slots = jnp.dot(
        held.astype(jnp.bfloat16), repeat, preferred_element_type=jnp.float32
    )
    owner_row = lax.broadcasted_iota(jnp.int32, (owners, nslot), 0)
    lane_owner = lax.broadcasted_iota(jnp.int32, (owners, nslot), 1) // per
    slot_row = jnp.sum(
        jnp.where(owner_row == lane_owner, wide_slots, 0.0), axis=0, keepdims=True
    ).astype(jnp.int32)
    full = jnp.where(held >= 0.0, 1.0, 0.0).astype(jnp.bfloat16)
    slot_of = lax.broadcasted_iota(jnp.int32, (per, LANES), 0)
    lane = lax.broadcasted_iota(jnp.int32, (per, LANES), 1)
    for j in range(ns):
        spot = jnp.where(slot_of == j * mine + (lane // NB) % mine, 1.0, 0.0)
        filled[j] = jnp.dot(
            full, spot.astype(jnp.bfloat16), preferred_element_type=jnp.float32
        )
    bin_of = lax.broadcasted_iota(jnp.int32, (wide, ntri), 0) // 2
    hit = (triads[0:1] == bin_of) | (triads[1:2] == bin_of) | (triads[2:3] == bin_of)
    hit = jnp.where(hit, 1.0, 0.0).astype(jnp.bfloat16)
    ones = jnp.ones((16, ntri), jnp.bfloat16)
    hits = lax.dot_general(
        ones, hit, (((1,), (1,)), ((), ())), preferred_element_type=jnp.float32
    )
    used = jnp.where(hits > 0.5, 1.0, 0.0)
    row = lax.broadcasted_iota(jnp.int32, (wide, wide), 0)
    column = lax.broadcasted_iota(jnp.int32, (wide, wide), 1)
    before = jnp.where(row < column, 1.0, 0.0).astype(jnp.bfloat16)
    rank = jnp.dot(used.astype(jnp.bfloat16), before, preferred_element_type=jnp.float32)
    place = jnp.where(used > 0.5, rank, -1.0)[0:1].astype(jnp.int32)
    pick = jnp.where(row == place, 1.0, 0.0).astype(jnp.bfloat16)
    chosen[...] = jnp.dot(
        pick, table[...], preferred_element_type=jnp.float32
    ).astype(jnp.bfloat16)
    triad_row = lax.broadcasted_iota(jnp.int32, (ntri, nslot), 0)
    of_slot = jnp.where(triad_row == slot_row, 1.0, 0.0).astype(jnp.bfloat16)
    bin_row = lax.broadcasted_iota(jnp.int32, (wide, nslot), 0)
    rank = rank.astype(jnp.bfloat16)
    for i in range(3):
        tri = jnp.broadcast_to(triads[i : i + 1].astype(jnp.float32), (16, ntri))
        freq = jnp.dot(
            tri.astype(jnp.bfloat16), of_slot, preferred_element_type=jnp.float32
        )
        same = bin_row == 2 * freq[0:1].astype(jnp.int32)
        same = jnp.where(same, 1.0, 0.0).astype(jnp.bfloat16)
        twice = jnp.dot(rank, same, preferred_element_type=jnp.float32)
        freqs[i : i + 1, :] = (twice[0:1] * 0.5).astype(jnp.int32)
    count[0, 0] = (jnp.sum(used[0:1]) * 0.5).astype(jnp.int32)


def kernel(
    n,
    ns,
    weight_scale,
    bins,
    snap,
    table,
    weights,
    freqs,
    filled,
    out,
    local,
    stage,
    recv,
    rows,
    spec,
    narrow,
    acc,
    part,
    summed,
    last,
    send_sem,
    recv_sem,
    own_sem,
    send1,
    recv1,
    send2,
    recv2,
):
    comps, times = snap.shape[0], snap.shape[1]
    me = lax.axis_index("tm")
    col = lax.axis_index("space")
    first = times % NT == 0
    blocks = times // NT

    def partner(place, m, size):
        other, bit = 0, 1
        while bit < size:
            other = other + lax.rem(place // bit + m // bit, 2) * bit
            bit *= 2
        return other

    def turn(i):
        i = lax.rem(i + lax.rem(col, 2) * (n // 2), n - 1)
        return (i + 1) // 2 + (1 - lax.rem(i, 2)) * (n // 2)

    def load(c):
        return pltpu.make_async_copy(snap.at[c], local.at[c], own_sem.at[c])

    if first:
        for c in range(comps):
            load(c).start()

    barrier = pltpu.get_barrier_semaphore()

    def greet_tm(off, carry):
        pl.semaphore_signal(
            barrier, inc=1, device_id=(partner(me, off, n), col), device_id_type=MESH
        )
        return carry

    lax.fori_loop(1, n, greet_tm, 0)
    for off in range(1, ns):
        pl.semaphore_signal(
            barrier, inc=1, device_id=(me, partner(col, off, ns)), device_id_type=MESH
        )
    pl.semaphore_wait(barrier, n - 1 + ns - 1)

    def exchange(c, off):
        peer = partner(me, off, n)
        if first:
            return pltpu.make_async_remote_copy(
                src_ref=stage.at[c, off],
                dst_ref=recv.at[c, off],
                send_sem=send_sem.at[c, off],
                recv_sem=recv_sem.at[c, off],
                device_id=(peer, col),
                device_id_type=MESH,
            )
        return pltpu.make_async_remote_copy(
            src_ref=snap.at[c, :, pl.ds(pl.multiple_of(peer * LANES, LANES), LANES)],
            dst_ref=recv.at[c, pl.ds(pl.multiple_of(me * times, 16), times), :],
            send_sem=send_sem.at[c, off],
            recv_sem=recv_sem.at[c, off],
            device_id=(peer, col),
            device_id_type=MESH,
        )

    def own(c):
        return pltpu.make_async_copy(
            snap.at[c, :, pl.ds(pl.multiple_of(me * LANES, LANES), LANES)],
            recv.at[c, pl.ds(pl.multiple_of(me * times, 16), times), :],
            own_sem.at[c],
        )

    def spectra(c, off):
        peer = partner(me, off, n)
        for i in range(blocks):
            x = local[
                c, i * NT : (i + 1) * NT, pl.ds(pl.multiple_of(peer * LANES, LANES), LANES)
            ]
            y = jnp.dot(table[: 2 * bins], x, preferred_element_type=jnp.float32)
            stage[c, off, i] = y.astype(jnp.bfloat16)

    for c in range(comps):
        if first:
            load(c).wait()

        def begin(i, carry, c=c):
            off = turn(i)
            if first:
                spectra(c, off)
            exchange(c, off).start()
            return carry

        lax.fori_loop(0, n - 1, begin, 0)
        if not first:
            own(c).start()

    w_row = weights[pl.ds(me, 1), :] * weight_scale
    lane = lax.broadcasted_iota(jnp.int32, (2 * NB, 2 * LANES), 1)
    lane_group = lax.rem(lane, LANES) // NB
    low = lax.broadcasted_iota(jnp.int32, (NB, LANES), 1) < LANES // 2
    groups = freqs.shape[1] // GROUP
    per_owner = groups // n

    def dft(c, b):
        x = recv[c, pl.ds(pl.multiple_of(b * NT, NT), NT), :]
        y = jnp.dot(table[...], x, preferred_element_type=jnp.float32)
        rows[pl.ds(b, 2 * K, stride=NB), :] = y

    def regroup(k, carry):
        both = rows[pl.ds(pl.multiple_of(k * 2 * NB, 2 * NB), 2 * NB), :].astype(jnp.bfloat16)
        narrow[k] = both
        spec[k] = both.astype(jnp.float32)
        return carry

    def spread(c, off, source):
        src = partner(me, off, n)
        for i in range(blocks):
            rows[pl.ds(src * blocks + i, 2 * bins, stride=NB), :] = source[c, off, i].astype(
                jnp.float32
            )

    def gram_group(c, owner, half):
        g = owner * per_owner + half
        prods, c_re, c_im = [], [], []
        for s in range(GROUP):
            place = g * GROUP + s
            a = spec[freqs[0, place]]
            b2 = spec[freqs[1, place]]
            c2 = narrow[freqs[2, place]]
            re = (a[:NB] * b2[:NB] - a[NB:] * b2[NB:]) * w_row
            im = (a[:NB] * b2[NB:] + a[NB:] * b2[:NB]) * w_row
            prods += [re.astype(jnp.bfloat16), im.astype(jnp.bfloat16)]
            c_re.append(c2[:NB])
            c_im.append(c2[NB:])
        left = jnp.concatenate(prods, axis=0)
        right = jnp.concatenate(c_re + c_im, axis=0)
        gram = lax.dot_general(
            left, right, (((1,), (1,)), ((), ())), preferred_element_type=jnp.float32
        )
        diag = gram[: 2 * NB]
        for s in range(1, GROUP):
            diag = jnp.where(lane_group == s, gram[2 * NB * s : 2 * NB * (s + 1)], diag)
        real = diag[:NB, :LANES] + diag[NB:, LANES:]
        imag = diag[:NB, LANES:] - diag[NB:, :LANES]
        half_turn = LANES // 2
        even = jnp.where(low, real, pltpu.roll(imag, half_turn, 1))
        odd = jnp.where(low, pltpu.roll(real, half_turn, 1), imag)
        if c == 0:
            acc[2 * half, owner] = even
            acc[2 * half + 1, owner] = odd
        else:
            acc[2 * half, owner] += even
            acc[2 * half + 1, owner] += odd

    def across(off):
        peer = partner(col, off, ns)
        return pltpu.make_async_remote_copy(
            src_ref=acc.at[peer],
            dst_ref=part.at[off - 1],
            send_sem=send1.at[off - 1],
            recv_sem=recv1.at[off - 1],
            device_id=(me, peer),
            device_id_type=MESH,
        )

    for c in range(comps):
        if first:
            spectra(c, 0)
            spread(c, 0, stage)

            def arrive(i, carry, c=c):
                off = turn(i)
                exchange(c, off).wait_recv()
                spread(c, off, recv)
                return carry

            lax.fori_loop(0, n - 1, arrive, 0)
        else:
            own(c).wait()

            def arrive(off, carry, c=c):
                exchange(c, off).wait_recv()
                return carry

            lax.fori_loop(1, n, arrive, 0)

            def transform(b, carry, c=c):
                dft(c, b)
                return carry

            lax.fori_loop(0, NB, transform, 0)

        lax.fori_loop(0, bins, regroup, 0, unroll=4)

        for j in range(per_owner):
            half = lax.rem(col // 2 + 1 + j, per_owner)

            def grams(owner, carry, c=c, half=half):
                gram_group(c, owner, half)
                return carry

            lax.fori_loop(0, n, grams, 0)
            if c == comps - 1:
                for off in (2, 3) if j == 0 else (1,):
                    across(off).start()

    for off in range(1, ns):
        across(off).wait_recv()
    total = acc[col]
    for off in range(1, ns):
        total = total + part[off - 1]
    summed[...] = total

    def along(off):
        peer = partner(me, off, n)
        return pltpu.make_async_remote_copy(
            src_ref=summed.at[peer],
            dst_ref=last.at[off],
            send_sem=send2.at[off],
            recv_sem=recv2.at[off],
            device_id=(peer, col),
            device_id_type=MESH,
        )

    def begin2(off, carry):
        along(off).start()
        return carry

    lax.fori_loop(1, n, begin2, 0)

    def add2(off, total):
        along(off).wait_recv()
        return total + last[off]

    summed_all = lax.fori_loop(1, n, add2, summed[me])
    out[...] = summed_all * filled[col, pl.ds(me, 1), :]

    for off in range(1, ns):
        across(off).wait_send()

    def drain(off, carry):
        for c in range(comps):
            exchange(c, off).wait_send()
        along(off).wait_send()
        return carry

    lax.fori_loop(1, n, drain, 0)


def shards(n, ns, snapshots, cell_weights, triads, owner_slots):
    times, comps, cells = snapshots.shape
    owners, slot_count = owner_slots.shape
    weight_scale = 1.0 / math.sqrt(comps * cells * ns)
    vmem = pl.BlockSpec(memory_space=pltpu.VMEM)
    smem = pl.BlockSpec(memory_space=pltpu.SMEM)
    anywhere = pl.BlockSpec(memory_space=pl.ANY)
    sem = pltpu.SemaphoreType.DMA
    first = times % NT == 0
    blocks = times // NT

    def call(which, bins, *operands):
        if first:
            local = pltpu.VMEM((comps, times, n * LANES), jnp.bfloat16)
            stage = pltpu.VMEM((comps, n, blocks, 2 * bins, LANES), jnp.bfloat16)
            recv = stage
        else:
            local = stage = pltpu.VMEM((16, LANES), jnp.bfloat16)
            recv = pltpu.VMEM((comps, NB * NT, LANES), jnp.bfloat16)
        return pl.pallas_call(
            functools.partial(kernel, n, ns, weight_scale, bins),
            out_shape=jax.ShapeDtypeStruct((NB, LANES), jnp.float32),
            in_specs=[anywhere, vmem, vmem, smem, vmem],
            out_specs=vmem,
            scratch_shapes=[
                local,
                stage,
                recv,
                pltpu.VMEM((2 * bins * NB, LANES), jnp.float32),
                pltpu.VMEM((bins, 2 * NB, LANES), jnp.float32),
                pltpu.VMEM((bins, 2 * NB, LANES), jnp.bfloat16),
                pltpu.VMEM((ns, n, NB, LANES), jnp.float32),
                pltpu.VMEM((ns - 1, n, NB, LANES), jnp.float32),
                pltpu.VMEM((n, NB, LANES), jnp.float32),
                pltpu.VMEM((n, NB, LANES), jnp.float32),
                sem((comps, n)),
                sem((comps, n)),
                sem((comps,)),
                sem((ns - 1,)),
                sem((ns - 1,)),
                sem((n,)),
                sem((n,)),
            ],
            compiler_params=pltpu.CompilerParams(
                collective_id=which,
                has_side_effects=True,
                vmem_limit_bytes=58 * 1024 * 1024,
            ),
        )(*operands)

    table = jnp.asarray(spectral_table())
    snap = snapshots.transpose(1, 0, 2)
    weights = cell_weights.reshape(n, LANES)
    mine = slot_count // ns
    if first:
        sizes = (96, 104, K)
        chosen, freqs, filled, count = pl.pallas_call(
            functools.partial(choose, ns),
            out_shape=(
                jax.ShapeDtypeStruct((2 * K, NT), jnp.bfloat16),
                jax.ShapeDtypeStruct((3, owners * slot_count), jnp.int32),
                jax.ShapeDtypeStruct((ns, owners, LANES), jnp.float32),
                jax.ShapeDtypeStruct((1, 1), jnp.int32),
            ),
            in_specs=[vmem, vmem, vmem],
            out_specs=(vmem, vmem, vmem, smem),
        )(table, triads.T, owner_slots)
        need = count[0, 0]
        which = (need > sizes[0]).astype(jnp.int32) + (need > sizes[1]).astype(jnp.int32)
        tile = lax.switch(
            which,
            [functools.partial(call, i, bins) for i, bins in enumerate(sizes)],
            snap,
            chosen,
            weights,
            freqs,
            filled,
        )
    else:
        flat = owner_slots.reshape(-1)
        freqs = jnp.take(triads.T, jnp.maximum(flat, 0), axis=1, mode="clip")
        filled = (owner_slots >= 0).astype(jnp.float32).reshape(owners, ns, mine)
        filled = jnp.tile(jnp.repeat(filled.transpose(1, 0, 2), NB, axis=2), (1, 1, 2))
        tile = call(0, K, snap, table, weights, freqs, filled)
    return (
        tile.reshape(NB, 2, mine, NB).transpose(2, 1, 0, 3).reshape(mine, 2 * NB * NB)
    )


def solution(mesh):
    placed = (P("tm", None, "space"), P("space"), P(), P())
    n, ns = mesh.shape["tm"], mesh.shape["space"]
    return jax.shard_map(
        functools.partial(shards, n, ns),
        mesh=mesh,
        in_specs=placed,
        out_specs=P(("tm", "space"), None),
        check_vma=False,
    )
```

```python
import functools
import math

import jax
import jax.numpy as jnp
import ml_dtypes
import numpy as np
from jax import lax
from jax.experimental import pallas as pl
from jax.experimental.pallas import tpu as pltpu
from jax.sharding import PartitionSpec as P

NB = 16
NT = 256
K = 128
GROUP = 8
LANES = 128
MESH = pl.DeviceIdType.MESH


def spectral_table():
    sample = np.arange(NT)
    freq_bins = np.arange(K)
    angles = 2.0 * math.pi / NT * (freq_bins[:, None] * sample[None, :] % NT)
    window = 0.5 - 0.5 * np.cos(2.0 * math.pi / NT * sample)
    scale = math.sqrt(8.0 / (3.0 * NT))
    rows = np.stack(
        [scale * window * np.cos(angles), -scale * window * np.sin(angles)], axis=1
    )
    return rows.reshape(2 * K, NT).astype(np.float32).astype(ml_dtypes.bfloat16)


def choose(ns, sizes, triads, slots, place, freqs, filled, which):
    wide = 2 * K
    ntri = triads.shape[1]
    owners, per = slots.shape
    nslot = owners * per
    mine = per // ns
    slot_of = lax.broadcasted_iota(jnp.int32, (per, nslot), 0)
    lane = lax.broadcasted_iota(jnp.int32, (per, nslot), 1)
    repeat = jnp.where(lane % per == slot_of, 1.0, 0.0).astype(jnp.bfloat16)
    held = slots[...].astype(jnp.float32)
    wide_slots = jnp.dot(
        held.astype(jnp.bfloat16), repeat, preferred_element_type=jnp.float32
    )
    owner_row = lax.broadcasted_iota(jnp.int32, (owners, nslot), 0)
    lane_owner = lax.broadcasted_iota(jnp.int32, (owners, nslot), 1) // per
    slot_row = jnp.sum(
        jnp.where(owner_row == lane_owner, wide_slots, 0.0), axis=0, keepdims=True
    ).astype(jnp.int32)
    full = jnp.where(held >= 0.0, 1.0, 0.0).astype(jnp.bfloat16)
    slot_of = lax.broadcasted_iota(jnp.int32, (per, LANES), 0)
    lane = lax.broadcasted_iota(jnp.int32, (per, LANES), 1)
    for j in range(ns):
        spot = jnp.where(slot_of == j * mine + (lane // NB) % mine, 1.0, 0.0)
        filled[j] = jnp.dot(
            full, spot.astype(jnp.bfloat16), preferred_element_type=jnp.float32
        )
    bin_of = lax.broadcasted_iota(jnp.int32, (wide, ntri), 0) // 2
    hit = (triads[0:1] == bin_of) | (triads[1:2] == bin_of) | (triads[2:3] == bin_of)
    hit = jnp.where(hit, 1.0, 0.0).astype(jnp.bfloat16)
    ones = jnp.ones((16, ntri), jnp.bfloat16)
    hits = lax.dot_general(
        ones, hit, (((1,), (1,)), ((), ())), preferred_element_type=jnp.float32
    )
    used = jnp.where(hits > 0.5, 1.0, 0.0)
    row = lax.broadcasted_iota(jnp.int32, (wide, wide), 0)
    column = lax.broadcasted_iota(jnp.int32, (wide, wide), 1)
    before = jnp.where(row < column, 1.0, 0.0).astype(jnp.bfloat16)
    rank = jnp.dot(used.astype(jnp.bfloat16), before, preferred_element_type=jnp.float32)
    place[...] = jnp.where(used > 0.5, rank, -1.0)[0:1].astype(jnp.int32)
    triad_row = lax.broadcasted_iota(jnp.int32, (ntri, nslot), 0)
    of_slot = jnp.where(triad_row == slot_row, 1.0, 0.0).astype(jnp.bfloat16)
    bin_row = lax.broadcasted_iota(jnp.int32, (wide, nslot), 0)
    rank = rank.astype(jnp.bfloat16)
    for i in range(3):
        tri = jnp.broadcast_to(triads[i : i + 1].astype(jnp.float32), (16, ntri))
        freq = jnp.dot(
            tri.astype(jnp.bfloat16), of_slot, preferred_element_type=jnp.float32
        )
        same = bin_row == 2 * freq[0:1].astype(jnp.int32)
        same = jnp.where(same, 1.0, 0.0).astype(jnp.bfloat16)
        twice = jnp.dot(rank, same, preferred_element_type=jnp.float32)
        freqs[i : i + 1, :] = (twice[0:1] * 0.5).astype(jnp.int32)
    need = jnp.sum(used[0:1]) * 0.5
    branch = jnp.int32(0)
    for size in sizes[:-1]:
        branch = branch + (need > size + 0.5).astype(jnp.int32)
    which[0, 0] = branch


def kernel(
    n,
    ns,
    weight_scale,
    bins,
    snap,
    table,
    place,
    weights,
    freqs,
    filled,
    out,
    whole,
    picked,
    local,
    stage,
    recv,
    rows,
    spec,
    narrow,
    acc,
    part,
    summed,
    last,
    send_sem,
    recv_sem,
    own_sem,
    table_sem,
    send1,
    recv1,
    send2,
    recv2,
):
    comps, times = snap.shape[0], snap.shape[1]
    me = lax.axis_index("tm")
    col = lax.axis_index("space")
    first = times % NT == 0
    blocks = times // NT

    def partner(place, m, size):
        other, bit = 0, 1
        while bit < size:
            other = other + lax.rem(place // bit + m // bit, 2) * bit
            bit *= 2
        return other

    def turn(i):
        i = lax.rem(i + lax.rem(col, 2) * (n // 2), n - 1)
        return (i + 1) // 2 + (1 - lax.rem(i, 2)) * (n // 2)

    def load(c):
        return pltpu.make_async_copy(snap.at[c], local.at[c], own_sem.at[c])

    fetch = pltpu.make_async_copy(table, whole, table_sem)
    fetch.start()
    if first:
        for c in range(comps):
            load(c).start()

    barrier = pltpu.get_barrier_semaphore()

    def greet_tm(off, carry):
        pl.semaphore_signal(
            barrier, inc=1, device_id=(partner(me, off, n), col), device_id_type=MESH
        )
        return carry

    lax.fori_loop(1, n, greet_tm, 0)
    for off in range(1, ns):
        pl.semaphore_signal(
            barrier, inc=1, device_id=(me, partner(col, off, ns)), device_id_type=MESH
        )
    fetch.wait()
    if first:
        row = lax.broadcasted_iota(jnp.int32, picked.shape, 0)
        pick = jnp.where(row == place[...], 1.0, 0.0).astype(jnp.bfloat16)
        picked[...] = jnp.dot(
            pick, whole[...], preferred_element_type=jnp.float32
        ).astype(jnp.bfloat16)
    pl.semaphore_wait(barrier, n - 1 + ns - 1)

    def exchange(c, off):
        peer = partner(me, off, n)
        if first:
            return pltpu.make_async_remote_copy(
                src_ref=stage.at[c, off],
                dst_ref=recv.at[c, off],
                send_sem=send_sem.at[c, off],
                recv_sem=recv_sem.at[c, off],
                device_id=(peer, col),
                device_id_type=MESH,
            )
        return pltpu.make_async_remote_copy(
            src_ref=snap.at[c, :, pl.ds(pl.multiple_of(peer * LANES, LANES), LANES)],
            dst_ref=recv.at[c, pl.ds(pl.multiple_of(me * times, 16), times), :],
            send_sem=send_sem.at[c, off],
            recv_sem=recv_sem.at[c, off],
            device_id=(peer, col),
            device_id_type=MESH,
        )

    def own(c):
        return pltpu.make_async_copy(
            snap.at[c, :, pl.ds(pl.multiple_of(me * LANES, LANES), LANES)],
            recv.at[c, pl.ds(pl.multiple_of(me * times, 16), times), :],
            own_sem.at[c],
        )

    def spectra(c, off):
        peer = partner(me, off, n)
        parts = []
        for i in range(blocks):
            x = local[
                c, i * NT : (i + 1) * NT, pl.ds(pl.multiple_of(peer * LANES, LANES), LANES)
            ]
            y = jnp.dot(picked[...], x, preferred_element_type=jnp.float32)
            parts.append(y[: 2 * bins])
        stage[c, off] = jnp.concatenate(parts, axis=0).astype(jnp.bfloat16)

    for c in range(comps):
        if first:
            load(c).wait()

        def begin(i, carry, c=c):
            off = turn(i)
            if first:
                spectra(c, off)
            exchange(c, off).start()
            return carry

        lax.fori_loop(0, n - 1, begin, 0)
        if not first:
            own(c).start()

    w_row = weights[pl.ds(me, 1), :] * weight_scale
    lane = lax.broadcasted_iota(jnp.int32, (2 * NB, 2 * LANES), 1)
    lane_group = lax.rem(lane, LANES) // NB
    low = lax.broadcasted_iota(jnp.int32, (NB, LANES), 1) < LANES // 2
    groups = freqs.shape[1] // GROUP
    per_owner = groups // n

    def dft(c, b):
        x = recv[c, pl.ds(pl.multiple_of(b * NT, NT), NT), :]
        y = jnp.dot(whole[...], x, preferred_element_type=jnp.float32)
        rows[pl.ds(b, 2 * K, stride=NB), :] = y

    def regroup(k, carry):
        both = rows[pl.ds(pl.multiple_of(k * 2 * NB, 2 * NB), 2 * NB), :].astype(jnp.bfloat16)
        narrow[k] = both
        spec[k] = both.astype(jnp.float32)
        return carry

    def spread(c, off, source):
        src = partner(me, off, n)
        both = source[c, off].astype(jnp.float32)
        for i in range(blocks):
            part_rows = both[i * 2 * bins : (i + 1) * 2 * bins]
            rows[pl.ds(src * blocks + i, 2 * bins, stride=NB), :] = part_rows

    def gram_group(c, owner, half):
        g = owner * per_owner + half
        prods, c_re, c_im = [], [], []
        for s in range(GROUP):
            place = g * GROUP + s
            a = spec[freqs[0, place]]
            b2 = spec[freqs[1, place]]
            c2 = narrow[freqs[2, place]]
            re = (a[:NB] * b2[:NB] - a[NB:] * b2[NB:]) * w_row
            im = (a[:NB] * b2[NB:] + a[NB:] * b2[:NB]) * w_row
            prods += [re.astype(jnp.bfloat16), im.astype(jnp.bfloat16)]
            c_re.append(c2[:NB])
            c_im.append(c2[NB:])
        left = jnp.concatenate(prods, axis=0)
        right = jnp.concatenate(c_re + c_im, axis=0)
        gram = lax.dot_general(
            left, right, (((1,), (1,)), ((), ())), preferred_element_type=jnp.float32
        )
        diag = gram[: 2 * NB]
        for s in range(1, GROUP):
            diag = jnp.where(lane_group == s, gram[2 * NB * s : 2 * NB * (s + 1)], diag)
        real = diag[:NB, :LANES] + diag[NB:, LANES:]
        imag = diag[:NB, LANES:] - diag[NB:, :LANES]
        half_turn = LANES // 2
        even = jnp.where(low, real, pltpu.roll(imag, half_turn, 1))
        odd = jnp.where(low, pltpu.roll(real, half_turn, 1), imag)
        if c == 0:
            acc[2 * half, owner] = even
            acc[2 * half + 1, owner] = odd
        else:
            acc[2 * half, owner] += even
            acc[2 * half + 1, owner] += odd

    def across(off):
        peer = partner(col, off, ns)
        return pltpu.make_async_remote_copy(
            src_ref=acc.at[peer],
            dst_ref=part.at[off - 1],
            send_sem=send1.at[off - 1],
            recv_sem=recv1.at[off - 1],
            device_id=(me, peer),
            device_id_type=MESH,
        )

    for c in range(comps):
        if first:
            spectra(c, 0)
            spread(c, 0, stage)

            def arrive(i, carry, c=c):
                off = turn(i)
                exchange(c, off).wait_recv()
                spread(c, off, recv)
                return carry

            lax.fori_loop(0, n - 1, arrive, 0)
        else:
            own(c).wait()

            def arrive(off, carry, c=c):
                exchange(c, off).wait_recv()
                return carry

            lax.fori_loop(1, n, arrive, 0)

            def transform(b, carry, c=c):
                dft(c, b)
                return carry

            lax.fori_loop(0, NB, transform, 0)

        lax.fori_loop(0, bins, regroup, 0, unroll=4)

        for j in range(per_owner):
            half = lax.rem(col // 2 + 1 + j, per_owner)

            def grams(owner, carry, c=c, half=half):
                gram_group(c, owner, half)
                return carry

            lax.fori_loop(0, n, grams, 0, unroll=2)
            if c == comps - 1:
                for off in (2, 3) if j == 0 else (1,):
                    across(off).start()

    for off in range(1, ns):
        across(off).wait_recv()
    total = acc[col]
    for off in range(1, ns):
        total = total + part[off - 1]
    summed[...] = total

    def along(off):
        peer = partner(me, off, n)
        return pltpu.make_async_remote_copy(
            src_ref=summed.at[peer],
            dst_ref=last.at[off],
            send_sem=send2.at[off],
            recv_sem=recv2.at[off],
            device_id=(peer, col),
            device_id_type=MESH,
        )

    def begin2(off, carry):
        along(off).start()
        return carry

    lax.fori_loop(1, n, begin2, 0)

    def add2(off, total):
        along(off).wait_recv()
        return total + last[off]

    summed_all = lax.fori_loop(1, n, add2, summed[me])
    out[...] = summed_all * filled[col, pl.ds(me, 1), :]

    for off in range(1, ns):
        across(off).wait_send()

    def drain(off, carry):
        for c in range(comps):
            exchange(c, off).wait_send()
        along(off).wait_send()
        return carry

    lax.fori_loop(1, n, drain, 0)


def shards(n, ns, snapshots, cell_weights, triads, owner_slots):
    times, comps, cells = snapshots.shape
    owners, slot_count = owner_slots.shape
    weight_scale = 1.0 / math.sqrt(comps * cells * ns)
    vmem = pl.BlockSpec(memory_space=pltpu.VMEM)
    smem = pl.BlockSpec(memory_space=pltpu.SMEM)
    anywhere = pl.BlockSpec(memory_space=pl.ANY)
    sem = pltpu.SemaphoreType.DMA
    first = times % NT == 0
    blocks = times // NT

    def call(which, bins, *operands):
        if first:
            local = pltpu.VMEM((comps, times, n * LANES), jnp.bfloat16)
            stage = pltpu.VMEM((comps, n, blocks * 2 * bins, LANES), jnp.bfloat16)
            recv = stage
        else:
            local = stage = pltpu.VMEM((16, LANES), jnp.bfloat16)
            recv = pltpu.VMEM((comps, NB * NT, LANES), jnp.bfloat16)
        return pl.pallas_call(
            functools.partial(kernel, n, ns, weight_scale, bins),
            out_shape=jax.ShapeDtypeStruct((NB, LANES), jnp.float32),
            in_specs=[anywhere, anywhere, vmem, vmem, smem, vmem],
            out_specs=vmem,
            scratch_shapes=[
                pltpu.VMEM((2 * K, NT), jnp.bfloat16),
                pltpu.VMEM(((2 * bins + 15) // 16 * 16, NT), jnp.bfloat16),
                local,
                stage,
                recv,
                pltpu.VMEM((2 * bins * NB, LANES), jnp.float32),
                pltpu.VMEM((bins, 2 * NB, LANES), jnp.float32),
                pltpu.VMEM((bins, 2 * NB, LANES), jnp.bfloat16),
                pltpu.VMEM((ns, n, NB, LANES), jnp.float32),
                pltpu.VMEM((ns - 1, n, NB, LANES), jnp.float32),
                pltpu.VMEM((n, NB, LANES), jnp.float32),
                pltpu.VMEM((n, NB, LANES), jnp.float32),
                sem((comps, n)),
                sem((comps, n)),
                sem((comps,)),
                sem,
                sem((ns - 1,)),
                sem((ns - 1,)),
                sem((n,)),
                sem((n,)),
            ],
            compiler_params=pltpu.CompilerParams(
                collective_id=which,
                has_side_effects=True,
                vmem_limit_bytes=58 * 1024 * 1024,
            ),
        )(*operands)

    table = jnp.asarray(spectral_table())
    snap = snapshots.transpose(1, 0, 2)
    weights = cell_weights.reshape(n, LANES)
    mine = slot_count // ns
    if first:
        sizes = (92, 96, 100, 104, 108, K)
        place, freqs, filled, which = pl.pallas_call(
            functools.partial(choose, ns, sizes),
            out_shape=(
                jax.ShapeDtypeStruct((1, 2 * K), jnp.int32),
                jax.ShapeDtypeStruct((3, owners * slot_count), jnp.int32),
                jax.ShapeDtypeStruct((ns, owners, LANES), jnp.float32),
                jax.ShapeDtypeStruct((1, 1), jnp.int32),
            ),
            in_specs=[vmem, vmem],
            out_specs=(vmem, vmem, vmem, smem),
        )(triads.T, owner_slots)
        tile = lax.switch(
            which[0, 0],
            [functools.partial(call, i, bins) for i, bins in enumerate(sizes)],
            snap,
            table,
            place,
            weights,
            freqs,
            filled,
        )
    else:
        flat = owner_slots.reshape(-1)
        freqs = jnp.take(triads.T, jnp.maximum(flat, 0), axis=1, mode="clip")
        filled = (owner_slots >= 0).astype(jnp.float32).reshape(owners, ns, mine)
        filled = jnp.tile(jnp.repeat(filled.transpose(1, 0, 2), NB, axis=2), (1, 1, 2))
        place = jnp.zeros((1, 2 * K), jnp.int32)
        tile = call(0, K, snap, table, place, weights, freqs, filled)
    return (
        tile.reshape(NB, 2, mine, NB).transpose(2, 1, 0, 3).reshape(mine, 2 * NB * NB)
    )


def solution(mesh):
    placed = (P("tm", None, "space"), P("space"), P(), P())
    n, ns = mesh.shape["tm"], mesh.shape["space"]
    return jax.shard_map(
        functools.partial(shards, n, ns),
        mesh=mesh,
        in_specs=placed,
        out_specs=P(("tm", "space"), None),
        check_vma=False,
    )
```

```python
import functools
import math

import jax
import jax.numpy as jnp
import ml_dtypes
import numpy as np
from jax import lax
from jax.experimental import pallas as pl
from jax.experimental.pallas import tpu as pltpu
from jax.sharding import PartitionSpec as P

NB = 16
NT = 256
K = 128
GROUP = 8
LANES = 128
MESH = pl.DeviceIdType.MESH


def spectral_table():
    sample = np.arange(NT)
    freq_bins = np.arange(K)
    angles = 2.0 * math.pi / NT * (freq_bins[:, None] * sample[None, :] % NT)
    window = 0.5 - 0.5 * np.cos(2.0 * math.pi / NT * sample)
    scale = math.sqrt(8.0 / (3.0 * NT))
    rows = np.stack(
        [scale * window * np.cos(angles), -scale * window * np.sin(angles)], axis=1
    )
    return rows.reshape(2 * K, NT).astype(np.float32).astype(ml_dtypes.bfloat16)


def choose(ns, sizes, triads, slots, place, freqs, filled, which):
    wide = 2 * K
    ntri = triads.shape[1]
    owners, per = slots.shape
    nslot = owners * per
    mine = per // ns
    slot_of = lax.broadcasted_iota(jnp.int32, (per, nslot), 0)
    lane = lax.broadcasted_iota(jnp.int32, (per, nslot), 1)
    repeat = jnp.where(lane % per == slot_of, 1.0, 0.0).astype(jnp.bfloat16)
    held = slots[...].astype(jnp.float32)
    wide_slots = jnp.dot(
        held.astype(jnp.bfloat16), repeat, preferred_element_type=jnp.float32
    )
    owner_row = lax.broadcasted_iota(jnp.int32, (owners, nslot), 0)
    lane_owner = lax.broadcasted_iota(jnp.int32, (owners, nslot), 1) // per
    slot_row = jnp.sum(
        jnp.where(owner_row == lane_owner, wide_slots, 0.0), axis=0, keepdims=True
    ).astype(jnp.int32)
    full = jnp.where(held >= 0.0, 1.0, 0.0).astype(jnp.bfloat16)
    slot_of = lax.broadcasted_iota(jnp.int32, (per, LANES), 0)
    lane = lax.broadcasted_iota(jnp.int32, (per, LANES), 1)
    for j in range(ns):
        spot = jnp.where(slot_of == j * mine + (lane // NB) % mine, 1.0, 0.0)
        filled[j] = jnp.dot(
            full, spot.astype(jnp.bfloat16), preferred_element_type=jnp.float32
        )
    bin_of = lax.broadcasted_iota(jnp.int32, (wide, ntri), 0) // 2
    hit = (triads[0:1] == bin_of) | (triads[1:2] == bin_of) | (triads[2:3] == bin_of)
    hit = jnp.where(hit, 1.0, 0.0).astype(jnp.bfloat16)
    ones = jnp.ones((16, ntri), jnp.bfloat16)
    hits = lax.dot_general(
        ones, hit, (((1,), (1,)), ((), ())), preferred_element_type=jnp.float32
    )
    used = jnp.where(hits > 0.5, 1.0, 0.0)
    row = lax.broadcasted_iota(jnp.int32, (wide, wide), 0)
    column = lax.broadcasted_iota(jnp.int32, (wide, wide), 1)
    before = jnp.where(row < column, 1.0, 0.0).astype(jnp.bfloat16)
    rank = jnp.dot(used.astype(jnp.bfloat16), before, preferred_element_type=jnp.float32)
    place[...] = jnp.where(used > 0.5, rank, -1.0)[0:1].astype(jnp.int32)
    triad_row = lax.broadcasted_iota(jnp.int32, (ntri, nslot), 0)
    of_slot = jnp.where(triad_row == slot_row, 1.0, 0.0).astype(jnp.bfloat16)
    bin_row = lax.broadcasted_iota(jnp.int32, (wide, nslot), 0)
    rank = rank.astype(jnp.bfloat16)
    for i in range(3):
        tri = jnp.broadcast_to(triads[i : i + 1].astype(jnp.float32), (16, ntri))
        freq = jnp.dot(
            tri.astype(jnp.bfloat16), of_slot, preferred_element_type=jnp.float32
        )
        same = bin_row == 2 * freq[0:1].astype(jnp.int32)
        same = jnp.where(same, 1.0, 0.0).astype(jnp.bfloat16)
        twice = jnp.dot(rank, same, preferred_element_type=jnp.float32)
        freqs[i : i + 1, :] = (twice[0:1] * 0.5).astype(jnp.int32)
    need = jnp.sum(used[0:1]) * 0.5
    branch = jnp.int32(0)
    for size in sizes[:-1]:
        branch = branch + (need > size + 0.5).astype(jnp.int32)
    which[0, 0] = branch


def kernel(
    n,
    ns,
    weight_scale,
    bins,
    snap,
    table,
    place,
    weights,
    freqs,
    filled,
    out,
    whole,
    picked,
    local,
    stage,
    recv,
    rows,
    spec,
    narrow,
    acc,
    part,
    summed,
    last,
    send_sem,
    recv_sem,
    own_sem,
    table_sem,
    send1,
    recv1,
    send2,
    recv2,
):
    comps, times = snap.shape[0], snap.shape[1]
    me = lax.axis_index("tm")
    col = lax.axis_index("space")
    first = times % NT == 0
    blocks = times // NT

    def partner(place, m, size):
        other, bit = 0, 1
        while bit < size:
            other = other + lax.rem(place // bit + m // bit, 2) * bit
            bit *= 2
        return other

    def turn(i):
        i = lax.rem(i + lax.rem(col, 2) * (n // 2), n - 1)
        return (i + 1) // 2 + (1 - lax.rem(i, 2)) * (n // 2)

    def load(c):
        return pltpu.make_async_copy(snap.at[c], local.at[c], own_sem.at[c])

    fetch = pltpu.make_async_copy(table, whole, table_sem)
    fetch.start()
    if first:
        for c in range(comps):
            load(c).start()

    barrier = pltpu.get_barrier_semaphore()

    def greet_tm(off, carry):
        pl.semaphore_signal(
            barrier, inc=1, device_id=(partner(me, off, n), col), device_id_type=MESH
        )
        return carry

    lax.fori_loop(1, n, greet_tm, 0)
    for off in range(1, ns):
        pl.semaphore_signal(
            barrier, inc=1, device_id=(me, partner(col, off, ns)), device_id_type=MESH
        )
    fetch.wait()
    if first:
        row = lax.broadcasted_iota(jnp.int32, picked.shape, 0)
        pick = jnp.where(row == place[...], 1.0, 0.0).astype(jnp.bfloat16)
        picked[...] = jnp.dot(
            pick, whole[...], preferred_element_type=jnp.float32
        ).astype(jnp.bfloat16)
    pl.semaphore_wait(barrier, n - 1 + ns - 1)

    def exchange(c, off):
        peer = partner(me, off, n)
        if first:
            return pltpu.make_async_remote_copy(
                src_ref=stage.at[c, off],
                dst_ref=recv.at[c, off],
                send_sem=send_sem.at[c, off],
                recv_sem=recv_sem.at[c, off],
                device_id=(peer, col),
                device_id_type=MESH,
            )
        return pltpu.make_async_remote_copy(
            src_ref=snap.at[c, :, pl.ds(pl.multiple_of(peer * LANES, LANES), LANES)],
            dst_ref=recv.at[c, pl.ds(pl.multiple_of(me * times, 16), times), :],
            send_sem=send_sem.at[c, off],
            recv_sem=recv_sem.at[c, off],
            device_id=(peer, col),
            device_id_type=MESH,
        )

    def own(c):
        return pltpu.make_async_copy(
            snap.at[c, :, pl.ds(pl.multiple_of(me * LANES, LANES), LANES)],
            recv.at[c, pl.ds(pl.multiple_of(me * times, 16), times), :],
            own_sem.at[c],
        )

    def spectra(c, off):
        peer = partner(me, off, n)
        parts = []
        for i in range(blocks):
            x = local[
                c, i * NT : (i + 1) * NT, pl.ds(pl.multiple_of(peer * LANES, LANES), LANES)
            ]
            y = jnp.dot(picked[...], x, preferred_element_type=jnp.float32)
            parts.append(y[: 2 * bins])
        stage[c, off] = jnp.concatenate(parts, axis=0).astype(jnp.bfloat16)

    for c in range(comps):
        if first:
            load(c).wait()

        def begin(i, carry, c=c):
            off = turn(i)
            if first:
                spectra(c, off)
            exchange(c, off).start()
            return carry

        lax.fori_loop(0, n - 1, begin, 0)
        if not first:
            own(c).start()

    w_row = weights[pl.ds(me, 1), :] * weight_scale
    lane = lax.broadcasted_iota(jnp.int32, (2 * NB, 2 * LANES), 1)
    lane_group = lax.rem(lane, LANES) // NB
    low = lax.broadcasted_iota(jnp.int32, (NB, LANES), 1) < LANES // 2
    groups = freqs.shape[1] // GROUP
    per_owner = groups // n

    def dft(c, b):
        x = recv[c, pl.ds(pl.multiple_of(b * NT, NT), NT), :]
        y = jnp.dot(whole[...], x, preferred_element_type=jnp.float32)
        rows[pl.ds(b, 2 * K, stride=NB), :] = y

    def regroup(k, carry):
        both = rows[pl.ds(pl.multiple_of(k * 2 * NB, 2 * NB), 2 * NB), :].astype(jnp.bfloat16)
        narrow[k] = both
        spec[k] = both.astype(jnp.float32)
        return carry

    def spread(c, off, source):
        src = partner(me, off, n)
        both = source[c, off].astype(jnp.float32)
        for i in range(blocks):
            part_rows = both[i * 2 * bins : (i + 1) * 2 * bins]
            rows[pl.ds(src * blocks + i, 2 * bins, stride=NB), :] = part_rows

    def gram_group(c, owner, half):
        g = owner * per_owner + half
        prods, c_re, c_im = [], [], []
        for s in range(GROUP):
            place = g * GROUP + s
            a = spec[freqs[0, place]]
            b2 = spec[freqs[1, place]]
            c2 = narrow[freqs[2, place]]
            re = (a[:NB] * b2[:NB] - a[NB:] * b2[NB:]) * w_row
            im = (a[:NB] * b2[NB:] + a[NB:] * b2[:NB]) * w_row
            prods += [re.astype(jnp.bfloat16), im.astype(jnp.bfloat16)]
            c_re.append(c2[:NB])
            c_im.append(c2[NB:])
        left = jnp.concatenate(prods, axis=0)
        right = jnp.concatenate(c_re + c_im, axis=0)
        gram = lax.dot_general(
            left, right, (((1,), (1,)), ((), ())), preferred_element_type=jnp.float32
        )
        diag = gram[: 2 * NB]
        for s in range(1, GROUP):
            diag = jnp.where(lane_group == s, gram[2 * NB * s : 2 * NB * (s + 1)], diag)
        real = diag[:NB, :LANES] + diag[NB:, LANES:]
        imag = diag[:NB, LANES:] - diag[NB:, :LANES]
        half_turn = LANES // 2
        even = jnp.where(low, real, pltpu.roll(imag, half_turn, 1))
        odd = jnp.where(low, pltpu.roll(real, half_turn, 1), imag)
        if c == 0:
            acc[2 * half, owner] = even
            acc[2 * half + 1, owner] = odd
        else:
            acc[2 * half, owner] += even
            acc[2 * half + 1, owner] += odd

    def across(off):
        peer = partner(col, off, ns)
        return pltpu.make_async_remote_copy(
            src_ref=acc.at[peer],
            dst_ref=part.at[off - 1],
            send_sem=send1.at[off - 1],
            recv_sem=recv1.at[off - 1],
            device_id=(me, peer),
            device_id_type=MESH,
        )

    for c in range(comps):
        if first:
            spectra(c, 0)
            spread(c, 0, stage)

            def arrive(i, carry, c=c):
                off = turn(i)
                exchange(c, off).wait_recv()
                spread(c, off, recv)
                return carry

            lax.fori_loop(0, n - 1, arrive, 0)
        else:
            own(c).wait()

            def arrive(off, carry, c=c):
                exchange(c, off).wait_recv()
                return carry

            lax.fori_loop(1, n, arrive, 0)

            def transform(b, carry, c=c):
                dft(c, b)
                return carry

            lax.fori_loop(0, NB, transform, 0)

        lax.fori_loop(0, bins, regroup, 0, unroll=4)

        for j in range(per_owner):
            half = lax.rem(col // 2 + 1 + j, per_owner)

            def grams(owner, carry, c=c, half=half):
                gram_group(c, owner, half)
                return carry

            lax.fori_loop(0, n, grams, 0, unroll=4)
            if c == comps - 1:
                for off in (2, 3) if j == 0 else (1,):
                    across(off).start()

    for off in range(1, ns):
        across(off).wait_recv()
    total = acc[col]
    for off in range(1, ns):
        total = total + part[off - 1]
    summed[...] = total

    def along(off):
        peer = partner(me, off, n)
        return pltpu.make_async_remote_copy(
            src_ref=summed.at[peer],
            dst_ref=last.at[off],
            send_sem=send2.at[off],
            recv_sem=recv2.at[off],
            device_id=(peer, col),
            device_id_type=MESH,
        )

    def begin2(off, carry):
        along(off).start()
        return carry

    lax.fori_loop(1, n, begin2, 0)

    def add2(off, total):
        along(off).wait_recv()
        return total + last[off]

    summed_all = lax.fori_loop(1, n, add2, summed[me])
    out[...] = summed_all * filled[col, pl.ds(me, 1), :]

    for off in range(1, ns):
        across(off).wait_send()

    def drain(off, carry):
        for c in range(comps):
            exchange(c, off).wait_send()
        along(off).wait_send()
        return carry

    lax.fori_loop(1, n, drain, 0)


def shards(n, ns, snapshots, cell_weights, triads, owner_slots):
    times, comps, cells = snapshots.shape
    owners, slot_count = owner_slots.shape
    weight_scale = 1.0 / math.sqrt(comps * cells * ns)
    vmem = pl.BlockSpec(memory_space=pltpu.VMEM)
    smem = pl.BlockSpec(memory_space=pltpu.SMEM)
    anywhere = pl.BlockSpec(memory_space=pl.ANY)
    sem = pltpu.SemaphoreType.DMA
    first = times % NT == 0
    blocks = times // NT

    def call(which, bins, *operands):
        if first:
            local = pltpu.VMEM((comps, times, n * LANES), jnp.bfloat16)
            stage = pltpu.VMEM((comps, n, blocks * 2 * bins, LANES), jnp.bfloat16)
            recv = stage
        else:
            local = stage = pltpu.VMEM((16, LANES), jnp.bfloat16)
            recv = pltpu.VMEM((comps, NB * NT, LANES), jnp.bfloat16)
        return pl.pallas_call(
            functools.partial(kernel, n, ns, weight_scale, bins),
            out_shape=jax.ShapeDtypeStruct((NB, LANES), jnp.float32),
            in_specs=[anywhere, anywhere, vmem, vmem, smem, vmem],
            out_specs=vmem,
            scratch_shapes=[
                pltpu.VMEM((2 * K, NT), jnp.bfloat16),
                pltpu.VMEM(((2 * bins + 15) // 16 * 16, NT), jnp.bfloat16),
                local,
                stage,
                recv,
                pltpu.VMEM((2 * bins * NB, LANES), jnp.float32),
                pltpu.VMEM((bins, 2 * NB, LANES), jnp.float32),
                pltpu.VMEM((bins, 2 * NB, LANES), jnp.bfloat16),
                pltpu.VMEM((ns, n, NB, LANES), jnp.float32),
                pltpu.VMEM((ns - 1, n, NB, LANES), jnp.float32),
                pltpu.VMEM((n, NB, LANES), jnp.float32),
                pltpu.VMEM((n, NB, LANES), jnp.float32),
                sem((comps, n)),
                sem((comps, n)),
                sem((comps,)),
                sem,
                sem((ns - 1,)),
                sem((ns - 1,)),
                sem((n,)),
                sem((n,)),
            ],
            compiler_params=pltpu.CompilerParams(
                collective_id=which,
                has_side_effects=True,
                vmem_limit_bytes=58 * 1024 * 1024,
            ),
        )(*operands)

    table = jnp.asarray(spectral_table())
    snap = snapshots.transpose(1, 0, 2)
    weights = cell_weights.reshape(n, LANES)
    mine = slot_count // ns
    if first:
        sizes = (92, 96, 100, 104, 108, K)
        place, freqs, filled, which = pl.pallas_call(
            functools.partial(choose, ns, sizes),
            out_shape=(
                jax.ShapeDtypeStruct((1, 2 * K), jnp.int32),
                jax.ShapeDtypeStruct((3, owners * slot_count), jnp.int32),
                jax.ShapeDtypeStruct((ns, owners, LANES), jnp.float32),
                jax.ShapeDtypeStruct((1, 1), jnp.int32),
            ),
            in_specs=[vmem, vmem],
            out_specs=(vmem, vmem, vmem, smem),
        )(triads.T, owner_slots)
        tile = lax.switch(
            which[0, 0],
            [functools.partial(call, i, bins) for i, bins in enumerate(sizes)],
            snap,
            table,
            place,
            weights,
            freqs,
            filled,
        )
    else:
        flat = owner_slots.reshape(-1)
        freqs = jnp.take(triads.T, jnp.maximum(flat, 0), axis=1, mode="clip")
        filled = (owner_slots >= 0).astype(jnp.float32).reshape(owners, ns, mine)
        filled = jnp.tile(jnp.repeat(filled.transpose(1, 0, 2), NB, axis=2), (1, 1, 2))
        place = jnp.zeros((1, 2 * K), jnp.int32)
        tile = call(0, K, snap, table, place, weights, freqs, filled)
    return (
        tile.reshape(NB, 2, mine, NB).transpose(2, 1, 0, 3).reshape(mine, 2 * NB * NB)
    )


def solution(mesh):
    placed = (P("tm", None, "space"), P("space"), P(), P())
    n, ns = mesh.shape["tm"], mesh.shape["space"]
    return jax.shard_map(
        functools.partial(shards, n, ns),
        mesh=mesh,
        in_specs=placed,
        out_specs=P(("tm", "space"), None),
        check_vma=False,
    )
```
